512 devices in a mesh: rows: 128 (over y_hi, x, z), cols: 4 (over y_lo, core).
Axes of the slice: x: 4, y: 4 (y_hi: 2, y_lo: 2; y = y_hi * 2 + y_lo), z: 16, core: 2. Of those that a mesh axis runs over, the one named last changes fastest.
Arguments:
- design_panel: float32 [128, 524288], P('cols', 'rows')
- sign_bits: int32 [524288], P('rows'), may hold values from 0 to 1
- sample_rows: int32 [512], replicated, may hold values from 0 to 524287
Outputs:
- conditioned: float32 [128, 524288], P('cols', 'rows')
The draws below stay inside these ranges and needn't reach their ends.
All inputs are finite; a program needn't handle non-finite values.
Results may differ from the reference program's by a relative error of at most 0.00015.
Values sent between devices are 32-bit elements; how exact they have to be, the bound alone decides.
A program may use at most 64 MiB of HBM per device.

```python
import math
import jax
import jax.numpy as jnp
from jax import lax

NCOL = 128
ROWS_DEV = 4096
SAMPLES = 512
PANEL_ROWS = 524288
N_ROWS = 128


def draw_design_panel(key, part):
    key = jax.random.fold_in(key, 11)
    key_col, key_row, key_base = jax.random.split(key, 3)
    col_scale = jnp.exp(jax.random.uniform(key_col, (NCOL, 1), jnp.float32) * math.log(10.0))
    row_scale = jnp.exp(jax.random.uniform(key_row, (1, PANEL_ROWS), jnp.float32) * math.log(10.0))
    base = jax.random.normal(key_base, (NCOL, PANEL_ROWS), jnp.float32)
    return base * col_scale * row_scale


def plant(values, own_key, smallest, largest):
    index_at = [jax.random.randint(jax.random.fold_in(own_key, axis), (), 0, length) for axis, length in enumerate(values.shape)]
    main_axis = values.shape.index(max(values.shape))
    neighbour = index_at[:main_axis] + [(index_at[main_axis] + 1) % values.shape[main_axis]] + index_at[main_axis + 1:]
    return values.at[tuple(index_at)].set(smallest).at[tuple(neighbour)].set(largest)


def setup_inputs(seed: int = 0) -> dict:
    splits = jax.random.split(jax.random.key(seed), 4)
    design_panel = draw_design_panel(jax.random.fold_in(splits[3], 71), 0)
    sign_bits = plant(jax.random.randint(splits[1], (PANEL_ROWS,), 0, 2), jax.random.fold_in(splits[1], 1), 0, 1).astype(jnp.int32)
    sample_rows = plant(jax.random.randint(splits[2], (SAMPLES,), 0, PANEL_ROWS), jax.random.fold_in(splits[2], 1), 0, PANEL_ROWS - 1).astype(jnp.int32)
    return dict(design_panel=design_panel, sign_bits=sign_bits, sample_rows=sample_rows)


precise = lax.Precision.HIGHEST

def sylvester(length):
    indices = jnp.arange(length, dtype=jnp.int32)
    common_bits = indices[:, None] & indices[None, :]
    parity = jnp.zeros((length, length), jnp.int32)
    for level in range(length.bit_length() - 1):
        parity = parity ^ common_bits >> level & 1
    return (1 - 2 * parity).astype(jnp.float32)

def reference(design_panel, sign_bits, sample_rows):
    total_rows = ROWS_DEV * N_ROWS
    blocks = ROWS_DEV // N_ROWS
    flipped = design_panel * (2 * sign_bits - 1).astype(jnp.float32)[None, :]
    cube_view = flipped.reshape(NCOL, N_ROWS, N_ROWS, blocks)
    outer_table = sylvester(N_ROWS)
    inner_table = sylvester(blocks)
    cube_view = jnp.einsum('cpjm,mn->cpjn', cube_view, inner_table, precision=precise)
    cube_view = jnp.einsum('cpjn,jk->cpkn', cube_view, outer_table, precision=precise)
    cube_view = jnp.einsum('cpkn,pq->cqkn', cube_view, outer_table, precision=precise)
    mixed_panel = cube_view.reshape(NCOL, total_rows) * (1.0 / jnp.sqrt(jnp.float32(total_rows)))
    picked = mixed_panel[:, sample_rows]
    gram_matrix = jnp.dot(picked, picked.T, precision=precise) / SAMPLES
    lower_factor = jnp.linalg.cholesky(gram_matrix)
    identity = jnp.eye(NCOL, dtype=jnp.float32)
    inverse = lax.linalg.triangular_solve(lower_factor, identity, left_side=True, lower=True)
    return jnp.dot(inverse, mixed_panel, precision=precise)
```

```python
import functools
import math

import jax
import jax.numpy as jnp
from jax import lax
from jax.experimental import pallas as pl
from jax.experimental.pallas import tpu as pltpu
from jax.sharding import PartitionSpec as P

MESH = pl.DeviceIdType.MESH
f32, bf16, i32 = jnp.float32, jnp.bfloat16, jnp.int32
HIGH = lax.Precision.HIGHEST
N_X, N_Z = 4, 16
PLANE = 8


def parity(value, bits):
    shift = bits // 2
    while shift:
        value = value ^ (value >> shift)
        shift //= 2
    return value & 1


def sylvester(n):
    rows = lax.broadcasted_iota(i32, (n, n), 0)
    cols = lax.broadcasted_iota(i32, (n, n), 1)
    return (1 - 2 * parity(rows & cols, 8)).astype(f32).astype(bf16)


def parts(value):
    high = value.astype(bf16)
    rest = value - high.astype(f32)
    middle = rest.astype(bf16)
    low = (rest - middle.astype(f32)).astype(bf16)
    return high, middle, low


def exact_dot(value, table):
    high, middle, low = parts(value)
    dot = functools.partial(jnp.dot, preferred_element_type=f32)
    return dot(low, table) + dot(middle, table) + dot(high, table)


def butterflies(tiles):
    n = tiles.shape[0]
    half = 1
    while half < n:
        pairs = tiles.reshape(n // (2 * half), 2, half, 8, 128)
        a, b = pairs[:, 0], pairs[:, 1]
        tiles = jnp.stack([a + b, a - b], axis=1).reshape(n, 8, 128)
        half *= 2
    return tiles


def wait_bytes(ref, sem):
    pltpu.make_async_copy(ref, ref, sem).wait()


def kernel(
    x_ref, sign_ref, sample_ref, out_ref,
    local, first, mixed, second, result,
    pick, pick_in, zsum, zsum_in, zrow, zall, picked, picked_all, factor,
    send_first, recv_first, send_second, recv_second, send_out, recv_out,
    chain_send, chain_recv, local_sem,
):
    p = lax.axis_index("rows")
    a = lax.axis_index("cols")
    z = lax.rem(p, N_Z)
    x = lax.rem(lax.div(p, N_Z), N_X)
    y = lax.div(p, N_Z * N_X)
    e = y * N_X + x
    quarter = lax.rem(x, 2) * 2 + lax.div(z, 8)
    slot = lax.rem(z, 8)
    block = y * 2 + lax.div(x, 2)

    def row_at(dz, de):
        zz = lax.rem(z + dz, N_Z)
        xx = lax.rem(x + lax.rem(de, N_X), N_X)
        yy = lax.rem(y + lax.div(de, N_X), 2)
        return (yy * N_X + xx) * N_Z + zz, yy * N_X + xx, zz

    def order(k):
        half = lax.rem(k, 2)
        de = lax.rem(lax.div(k, 2), PLANE)
        dz = lax.rem(3 * lax.div(k, 16), 8) + 8 * half
        return dz, de

    scale = f32(1.0 / math.sqrt(524288.0))
    signs = (2 * sign_ref[...] - 1).astype(f32) * scale
    table = sylvester(128)
    for cb in range(4):
        flipped = x_ref[cb * 8 : cb * 8 + 8, :] * signs
        tiles = jnp.concatenate([flipped[:, j * 128 : j * 128 + 128] for j in range(32)], axis=0)
        tiles = exact_dot(tiles, table).reshape(32, 8, 128)
        local[cb * 32 : cb * 32 + 32] = butterflies(tiles)

    def send_tile(k, carry):
        dz, de = order(k)
        row, _, _ = row_at(dz, de)
        pltpu.make_async_remote_copy(
            src_ref=local.at[row], dst_ref=first.at[p], send_sem=send_first, recv_sem=recv_first,
            device_id=(row, a), device_id_type=MESH,
        ).start()
        return carry

    lax.fori_loop(1, 128, send_tile, 0)
    first[p] = local[p]

    samples = sample_ref[...]
    hot = (lax.broadcasted_iota(i32, (128, 512), 0) == lax.rem(samples, 128)).astype(f32).astype(bf16)
    want = jnp.broadcast_to(lax.rem(lax.div(samples, 128), 32), (8, 512))
    flip = (1 - 2 * parity(lax.div(samples, 4096) & p, 8)).astype(f32)
    for cb in range(4):
        chosen = exact_dot(local[cb * 32 : cb * 32 + 32].reshape(256, 128), hot)
        total = jnp.zeros((8, 512), f32)
        for j in range(32):
            total = jnp.where(want == j, chosen[j * 8 : j * 8 + 8], total)
        total = total * flip
        for hf in range(2):
            for h in range(2):
                at = (hf * 2 + h) * 128
                pick[cb * 2 + hf, h] = total[:, at : at + 128]

    def send_pick(de, carry):
        row, ee, _ = row_at(0, de)
        pltpu.make_async_remote_copy(
            src_ref=pick.at[ee], dst_ref=pick_in.at[e], send_sem=chain_send.at[0], recv_sem=chain_recv.at[0],
            device_id=(row, a), device_id_type=MESH,
        ).start()
        return carry

    lax.fori_loop(1, PLANE, send_pick, 0)
    pick_in[e] = pick[e]
    wait_bytes(pick_in.at[pl.ds(0, PLANE - 1)], chain_recv.at[0])
    share = jnp.sum(pick_in[...], axis=0)
    for r in range(16):
        zsum[r] = share[r // 8, r % 8 : r % 8 + 1, :]

    def send_zsum(dz, carry):
        row, _, zz = row_at(dz, 0)
        pltpu.make_async_remote_copy(
            src_ref=zsum.at[zz], dst_ref=zsum_in.at[z], send_sem=chain_send.at[1], recv_sem=chain_recv.at[1],
            device_id=(row, a), device_id_type=MESH,
        ).start()
        return carry

    lax.fori_loop(1, N_Z, send_zsum, 0)
    zsum_in[z] = zsum[z]
    wait_bytes(zsum_in.at[pl.ds(0, N_Z - 1)], chain_recv.at[1])
    row_sum = jnp.sum(zsum_in[...], axis=0)
    zrow[0] = row_sum
    zall[z] = row_sum

    def send_zrow(dz, carry):
        row, _, _ = row_at(dz, 0)
        pltpu.make_async_remote_copy(
            src_ref=zrow.at[0], dst_ref=zall.at[z], send_sem=chain_send.at[2], recv_sem=chain_recv.at[2],
            device_id=(row, a), device_id_type=MESH,
        ).start()
        return carry

    lax.fori_loop(1, N_Z, send_zrow, 0)
    wait_bytes(zall.at[pl.ds(0, N_Z - 1)], chain_recv.at[2])
    for h in range(2):
        picked[h] = jnp.concatenate([zall[h * 8 + r] for r in range(8)], axis=0)

    mine = lax.rem(e, 2) * 16 + a * 4 + lax.div(e, 2)

    def send_picked(k, carry):
        row, _, _ = row_at(0, lax.rem(k, PLANE))
        col = lax.rem(a + lax.div(k, PLANE), 4)
        pltpu.make_async_remote_copy(
            src_ref=picked, dst_ref=picked_all.at[mine], send_sem=chain_send.at[3], recv_sem=chain_recv.at[3],
            device_id=(row, col), device_id_type=MESH,
        ).start()
        return carry

    lax.fori_loop(1, 32, send_picked, 0)
    picked_all[mine] = picked[...]

    wait_bytes(first.at[pl.ds(0, 127)], recv_first)
    for hi in range(PLANE):
        first[hi * 16 : hi * 16 + 16] = butterflies(first[hi * 16 : hi * 16 + 16])
    for lo in range(N_Z):
        tiles = butterflies(jnp.stack([first[hi * 16 + lo] for hi in range(PLANE)], axis=0))
        for hi in range(PLANE):
            mixed[hi * 16 + lo] = tiles[hi]

    def send_mixed(k, carry):
        dz, de = order(k)
        row, _, _ = row_at(dz, de)
        pltpu.make_async_remote_copy(
            src_ref=mixed.at[row], dst_ref=second.at[slot, a * 4 + block],
            send_sem=send_second, recv_sem=recv_second.at[slot],
            device_id=(row, quarter), device_id_type=MESH,
        ).start()
        return carry

    away = quarter != a

    @pl.when(away)
    def _():
        pltpu.make_async_remote_copy(
            src_ref=mixed.at[p], dst_ref=second.at[slot, a * 4 + block],
            send_sem=send_second, recv_sem=recv_second.at[slot],
            device_id=(p, quarter), device_id_type=MESH,
        ).start()

    @pl.when(jnp.logical_not(away))
    def _():
        pltpu.make_async_copy(mixed.at[p], second.at[slot, a * 4 + block], recv_second.at[slot]).start()

    lax.fori_loop(1, 128, send_mixed, 0)

    wait_bytes(picked_all.at[pl.ds(0, 31)], chain_recv.at[3])
    gram = jnp.zeros((128, 128), f32)
    for hf in range(2):
        for h in range(2):
            part = picked_all[hf * 16 : hf * 16 + 16, h].reshape(128, 128)
            gram = gram + lax.dot_general(
                part, part, (((1,), (1,)), ((), ())), precision=HIGH, preferred_element_type=f32
            )
    gram = gram * f32(1.0 / 512.0)
    rows = lax.broadcasted_iota(i32, (128, 128), 0)
    cols = lax.broadcasted_iota(i32, (128, 128), 1)
    eye = (rows == cols).astype(f32)
    rest = jnp.concatenate([gram, eye], axis=1)
    for b in range(16):
        place = lax.broadcasted_iota(i32, (128 - 8 * b, 1), 0)
        for r in range(8):
            k = b * 8 + r
            pivot_row = rest[r : r + 1, :]
            pivot_row = pivot_row * (1.0 / pivot_row[:, k : k + 1])
            below = jnp.where(place > r, rest[:, k : k + 1], 0.0)
            rest = rest - below * pivot_row
        done = rest[:8]
        pivots = jnp.sum(jnp.where(eye[b * 8 : b * 8 + 8] > 0, done[:, :128], 0.0), axis=1, keepdims=True)
        factor[b * 8 : b * 8 + 8] = done[:, 128:] * lax.rsqrt(pivots)
        rest = rest[8:]

    inverse = factor[...]

    def finish(step, carry):
        at = lax.rem(z + 16 - lax.rem(3 * step, 8), 8)
        wait_bytes(second.at[at], recv_second.at[at])
        value = jnp.dot(
            inverse, second[at].reshape(128, 128), precision=HIGH, preferred_element_type=f32
        )
        result[at] = value.reshape(4, 32, 128)
        start = pl.multiple_of((a * 8 + at) * 128, 128)
        for off in range(1, 4):
            col = lax.rem(a + off, 4)
            pltpu.make_async_remote_copy(
                src_ref=result.at[at, col], dst_ref=out_ref.at[:, pl.ds(start, 128)],
                send_sem=send_out, recv_sem=recv_out,
                device_id=(p, col), device_id_type=MESH,
            ).start()
        out_ref[:, pl.ds(start, 128)] = result[at, a]
        return carry

    lax.fori_loop(0, 8, finish, 0)

    wait_bytes(out_ref.at[:, pl.ds(0, 3072)], recv_out)
    wait_bytes(local.at[pl.ds(0, 127)], send_first)
    wait_bytes(mixed.at[pl.ds(0, 127)], send_second)

    @pl.when(away)
    def _():
        wait_bytes(mixed.at[0], send_second)

    wait_bytes(result.at[pl.ds(0, 6)], send_out)
    wait_bytes(pick.at[pl.ds(0, PLANE - 1)], chain_send.at[0])
    wait_bytes(zsum.at[pl.ds(0, N_Z - 1)], chain_send.at[1])
    wait_bytes(zall.at[pl.ds(0, N_Z - 1)], chain_send.at[2])
    wait_bytes(picked_all.at[pl.ds(0, 31)], chain_send.at[3])


def shards(design_panel, sign_bits, sample_rows):
    vmem = pl.BlockSpec(memory_space=pltpu.VMEM)
    tiles = pltpu.VMEM((128, 8, 128), f32)
    dma = pltpu.SemaphoreType.DMA
    return pl.pallas_call(
        kernel,
        out_shape=jax.ShapeDtypeStruct((32, 4096), f32),
        in_specs=[vmem] * 3,
        out_specs=vmem,
        scratch_shapes=[
            tiles, tiles, tiles,
            pltpu.VMEM((8, 16, 8, 128), f32),
            pltpu.VMEM((8, 4, 32, 128), f32),
            pltpu.VMEM((8, 2, 8, 128), f32),
            pltpu.VMEM((8, 2, 8, 128), f32),
            pltpu.VMEM((16, 1, 128), f32),
            pltpu.VMEM((16, 1, 128), f32),
            pltpu.VMEM((1, 1, 128), f32),
            pltpu.VMEM((16, 1, 128), f32),
            pltpu.VMEM((2, 8, 128), f32),
            pltpu.VMEM((32, 2, 8, 128), f32),
            pltpu.VMEM((128, 128), f32),
            dma(()), dma(()), dma(()), dma((8,)), dma(()), dma(()),
            dma((4,)), dma((4,)), dma(()),
        ],
        compiler_params=pltpu.CompilerParams(has_side_effects=True, vmem_limit_bytes=32 * 2**20),
        cost_estimate=pl.CostEstimate(flops=10**9, bytes_accessed=2**20, transcendentals=0),
    )(design_panel, sign_bits.reshape(1, 4096), sample_rows.reshape(1, 512))


def solution(mesh):
    return jax.shard_map(
        shards,
        mesh=mesh,
        in_specs=(P("cols", "rows"), P("rows"), P()),
        out_specs=P("cols", "rows"),
        check_vma=False,
    )
```

```python
import functools
import math

import jax
import jax.numpy as jnp
from jax import lax
from jax.experimental import pallas as pl
from jax.experimental.pallas import tpu as pltpu
from jax.sharding import PartitionSpec as P

MESH = pl.DeviceIdType.MESH
f32, bf16, i32 = jnp.float32, jnp.bfloat16, jnp.int32
HIGH = lax.Precision.HIGHEST
N_X, N_Z = 4, 16
PLANE = 8
CUT_A, CUT_B = 5, 10
EARLY = False


def parity(value, bits):
    shift = bits // 2
    while shift:
        value = value ^ (value >> shift)
        shift //= 2
    return value & 1


def sylvester(n):
    rows = lax.broadcasted_iota(i32, (n, n), 0)
    cols = lax.broadcasted_iota(i32, (n, n), 1)
    return (1 - 2 * parity(rows & cols, 8)).astype(f32).astype(bf16)


def parts(value):
    high = value.astype(bf16)
    rest = value - high.astype(f32)
    middle = rest.astype(bf16)
    low = (rest - middle.astype(f32)).astype(bf16)
    return high, middle, low


def exact_dot(value, table):
    high, middle, low = parts(value)
    dot = functools.partial(jnp.dot, preferred_element_type=f32)
    return dot(low, table) + dot(middle, table) + dot(high, table)


def butterflies(tiles):
    n = tiles.shape[0]
    half = 1
    while half < n:
        pairs = tiles.reshape(n // (2 * half), 2, half, 8, 128)
        a, b = pairs[:, 0], pairs[:, 1]
        tiles = jnp.stack([a + b, a - b], axis=1).reshape(n, 8, 128)
        half *= 2
    return tiles


def wait_bytes(ref, sem):
    pltpu.make_async_copy(ref, ref, sem).wait()


def kernel(
    x_hbm, sign_hbm, sample_hbm, out_ref,
    x_ref, sign_ref, sample_ref,
    local, first, mixed, second, result,
    pick, pick_in, zsum, zsum_in, zrow, zall, picked, picked_all, factor,
    load_sem, go_sem,
    send_first, recv_first, send_second, recv_second, send_out, recv_out,
    chain_send, chain_recv,
):
    loads = [
        pltpu.make_async_copy(source, target, load_sem.at[n])
        for n, (source, target) in enumerate(
            ((x_hbm, x_ref), (sign_hbm, sign_ref), (sample_hbm, sample_ref))
        )
    ]
    for load in loads:
        load.start()

    p = lax.axis_index("rows")
    a = lax.axis_index("cols")
    z = lax.rem(p, N_Z)
    x = lax.rem(lax.div(p, N_Z), N_X)
    y = lax.div(p, N_Z * N_X)
    e = y * N_X + x
    quarter = lax.rem(x, 2) * 2 + lax.div(z, 8)
    slot = lax.rem(z, 8)
    block = y * 2 + lax.div(x, 2)
    plane = []
    for de in range(PLANE):
        plane.append(lax.rem(y + de // N_X, 2) * N_X + lax.rem(x + de % N_X, N_X))
    base = [at * N_Z for at in plane]
    col = [a] + [lax.rem(a + k, 4) for k in range(1, 4)]

    def along(dz):
        return lax.rem(z + dz, N_Z)

    def far_first(i):
        return 8 + lax.div(i + 1, 2) * (1 - 2 * lax.rem(i, 2))

    def even(i):
        middle = lax.div(i + 1, 2)
        return lax.rem(8 + middle * (2 * lax.rem(i, 2) - 1), 8)

    def remote(source, target, send, recv, row, column):
        pltpu.make_async_remote_copy(
            src_ref=source, dst_ref=target, send_sem=send, recv_sem=recv,
            device_id=(row, column), device_id_type=MESH,
        ).start()

    def signal(sem, row, column):
        pl.semaphore_signal(sem, inc=1, device_id=(row, column), device_id_type=MESH)

    barrier = pltpu.get_barrier_semaphore()

    def greet(i, carry):
        signal(barrier, base[0] + along(far_first(i)), a)
        return carry

    lax.fori_loop(0, N_Z - 1, greet, 0, unroll=True)
    for de in range(1, PLANE):
        signal(barrier, base[de] + z, a)
    for k in range(1, 4):
        signal(barrier, p, col[k])

    for load in loads:
        load.wait()
    scale = f32(1.0 / math.sqrt(524288.0))
    signs = (2 * sign_ref[...] - 1).astype(f32) * scale
    table = sylvester(128)
    for cb in range(4):
        flipped = x_ref[cb * 8 : cb * 8 + 8, :] * signs
        tiles = jnp.concatenate([flipped[:, j * 128 : j * 128 + 128] for j in range(32)], axis=0)
        tiles = exact_dot(tiles, table).reshape(32, 8, 128)
        local[cb * 32 : cb * 32 + 32] = butterflies(tiles)

    samples = sample_ref[...]
    hot = (lax.broadcasted_iota(i32, (128, 512), 0) == lax.rem(samples, 128)).astype(f32).astype(bf16)
    want = jnp.broadcast_to(lax.rem(lax.div(samples, 128), 32), (8, 512))
    flip = (1 - 2 * parity(lax.div(samples, 4096) & p, 8)).astype(f32)
    for cb in range(4):
        chosen = exact_dot(local[cb * 32 : cb * 32 + 32].reshape(256, 128), hot)
        total = jnp.zeros((8, 512), f32)
        for j in range(32):
            total = jnp.where(want == j, chosen[j * 8 : j * 8 + 8], total)
        total = total * flip
        for hf in range(2):
            for h in range(2):
                at = (hf * 2 + h) * 128
                pick[cb * 2 + hf, h] = total[:, at : at + 128]

    pl.semaphore_wait(barrier, N_Z - 1 + PLANE - 1 + 3)

    def greet_again(i, carry):
        signal(go_sem, base[0] + along(far_first(i)), a)
        return carry

    lax.fori_loop(0, N_Z - 1, greet_again, 0, unroll=True)

    for de in range(1, PLANE):
        remote(pick.at[plane[de]], pick_in.at[e], chain_send.at[0], chain_recv.at[0], base[de] + z, a)

    def send_tile(row):
        remote(local.at[row], first.at[p], send_first, recv_first, row, a)

    def send_line(i, carry):
        send_tile(base[0] + along(far_first(i)))
        return carry

    def send_planes(i, carry):
        zz = along(far_first(i))
        for de in range(1, PLANE):
            send_tile(base[de] + zz)
        return carry

    lax.fori_loop(0, N_Z - 1, send_line, 0, unroll=True)
    pl.semaphore_wait(go_sem, N_Z - 1)
    lax.fori_loop(0, CUT_A, send_planes, 0)
    first[p] = local[p]
    pick_in[e] = pick[e]

    wait_bytes(pick_in.at[pl.ds(0, PLANE - 1)], chain_recv.at[0])
    share = jnp.sum(pick_in[...], axis=0)
    for r in range(16):
        zsum[r] = share[r // 8, r % 8 : r % 8 + 1, :]

    def send_zsum(i, carry):
        zz = along(far_first(i))
        remote(zsum.at[zz], zsum_in.at[z], chain_send.at[1], chain_recv.at[1], base[0] + zz, a)
        return carry

    lax.fori_loop(0, N_Z - 1, send_zsum, 0, unroll=True)
    zsum_in[z] = zsum[z]
    lax.fori_loop(CUT_A, CUT_B, send_planes, 0)
    wait_bytes(zsum_in.at[pl.ds(0, N_Z - 1)], chain_recv.at[1])
    row_sum = jnp.sum(zsum_in[...], axis=0)
    zrow[0] = row_sum
    zall[z] = row_sum

    def send_zrow(i, carry):
        remote(zrow.at[0], zall.at[z], chain_send.at[2], chain_recv.at[2], base[0] + along(far_first(i)), a)
        return carry

    lax.fori_loop(0, N_Z - 1, send_zrow, 0, unroll=True)
    lax.fori_loop(CUT_B, N_Z - 1, send_planes, 0)
    for de in range(1, PLANE):
        send_tile(base[de] + z)

    mine = lax.rem(e, 2) * 16 + a * 4 + lax.div(e, 2)

    def share_picked():
        wait_bytes(zall.at[pl.ds(0, N_Z - 1)], chain_recv.at[2])
        for h in range(2):
            picked[h] = jnp.concatenate([zall[h * 8 + r] for r in range(8)], axis=0)
        for de in range(PLANE):
            for k in range(4):
                if de or k:
                    remote(
                        picked, picked_all.at[mine], chain_send.at[3], chain_recv.at[3],
                        base[de] + z, col[k],
                    )
        picked_all[mine] = picked[...]

    if EARLY:
        share_picked()

    wait_bytes(first.at[pl.ds(0, 127)], recv_first)
    for hi in range(PLANE):
        first[hi * 16 : hi * 16 + 16] = butterflies(first[hi * 16 : hi * 16 + 16])
    target = second.at[slot, a * 4 + block]
    landed = recv_second.at[slot]
    away = quarter != a

    def mix_and_send(zz, own):
        tiles = butterflies(jnp.stack([first[hi * 16 + zz] for hi in range(PLANE)], axis=0))
        for hi in range(PLANE):
            mixed[hi * 16 + zz] = tiles[hi]
        for de in range(1 if own else 0, PLANE):
            remote(mixed.at[base[de] + zz], target, send_second, landed, base[de] + zz, quarter)

    def send_mixed(i, carry):
        mix_and_send(along(even(i)), False)
        mix_and_send(along(even(i) + 8), False)
        return carry

    mix_and_send(along(8), False)
    mix_and_send(z, True)

    @pl.when(away)
    def _():
        remote(mixed.at[p], target, send_second, landed, p, quarter)

    @pl.when(jnp.logical_not(away))
    def _():
        pltpu.make_async_copy(mixed.at[p], target, landed).start()

    lax.fori_loop(1, 8, send_mixed, 0)
    if not EARLY:
        share_picked()

    wait_bytes(picked_all.at[pl.ds(0, 31)], chain_recv.at[3])
    gram = jnp.zeros((128, 128), f32)
    for hf in range(2):
        for h in range(2):
            part = picked_all[hf * 16 : hf * 16 + 16, h].reshape(128, 128)
            gram = gram + lax.dot_general(
                part, part, (((1,), (1,)), ((), ())), precision=HIGH, preferred_element_type=f32
            )
    gram = gram * f32(1.0 / 512.0)
    rows = lax.broadcasted_iota(i32, (128, 128), 0)
    cols = lax.broadcasted_iota(i32, (128, 128), 1)
    eye = (rows == cols).astype(f32)
    rest = jnp.concatenate([gram, eye], axis=1)
    for b in range(16):
        place = lax.broadcasted_iota(i32, (128 - 8 * b, 1), 0)
        for r in range(8):
            k = b * 8 + r
            pivot_row = rest[r : r + 1, :]
            pivot_row = pivot_row * (1.0 / pivot_row[:, k : k + 1])
            below = jnp.where(place > r, rest[:, k : k + 1], 0.0)
            rest = rest - below * pivot_row
        done = rest[:8]
        pivots = jnp.sum(jnp.where(eye[b * 8 : b * 8 + 8] > 0, done[:, :128], 0.0), axis=1, keepdims=True)
        factor[b * 8 : b * 8 + 8] = done[:, 128:] * lax.rsqrt(pivots)
        rest = rest[8:]

    inverse = factor[...]

    def finish(step, carry):
        at = lax.rem(z + 8 - even(step), 8)
        wait_bytes(second.at[at], recv_second.at[at])
        value = jnp.dot(
            inverse, second[at].reshape(128, 128), precision=HIGH, preferred_element_type=f32
        )
        result[at] = value.reshape(4, 32, 128)
        start = pl.multiple_of((a * 8 + at) * 128, 128)
        there = out_ref.at[:, pl.ds(start, 128)]
        for k in range(1, 4):
            remote(result.at[at, col[k]], there, send_out, recv_out, p, col[k])
        pltpu.make_async_copy(result.at[at, a], there, recv_out).start()
        return carry

    lax.fori_loop(0, 8, finish, 0)

    wait_bytes(out_ref, recv_out)
    wait_bytes(local.at[pl.ds(0, 127)], send_first)
    wait_bytes(mixed.at[pl.ds(0, 127)], send_second)

    @pl.when(away)
    def _():
        wait_bytes(mixed.at[0], send_second)

    wait_bytes(result.at[pl.ds(0, 6)], send_out)
    wait_bytes(pick.at[pl.ds(0, PLANE - 1)], chain_send.at[0])
    wait_bytes(zsum.at[pl.ds(0, N_Z - 1)], chain_send.at[1])
    wait_bytes(zall.at[pl.ds(0, N_Z - 1)], chain_send.at[2])
    wait_bytes(picked_all.at[pl.ds(0, 31)], chain_send.at[3])


def shards(design_panel, sign_bits, sample_rows):
    anywhere = pl.BlockSpec(memory_space=pl.ANY)
    tiles = pltpu.VMEM((128, 8, 128), f32)
    dma = pltpu.SemaphoreType.DMA
    return pl.pallas_call(
        kernel,
        out_shape=jax.ShapeDtypeStruct((32, 4096), f32),
        in_specs=[anywhere] * 3,
        out_specs=anywhere,
        scratch_shapes=[
            pltpu.VMEM((32, 4096), f32),
            pltpu.VMEM((1, 4096), i32),
            pltpu.VMEM((1, 512), i32),
            tiles, tiles, tiles,
            pltpu.VMEM((8, 16, 8, 128), f32),
            pltpu.VMEM((8, 4, 32, 128), f32),
            pltpu.VMEM((8, 2, 8, 128), f32),
            pltpu.VMEM((8, 2, 8, 128), f32),
            pltpu.VMEM((16, 1, 128), f32),
            pltpu.VMEM((16, 1, 128), f32),
            pltpu.VMEM((1, 1, 128), f32),
            pltpu.VMEM((16, 1, 128), f32),
            pltpu.VMEM((2, 8, 128), f32),
            pltpu.VMEM((32, 2, 8, 128), f32),
            pltpu.VMEM((128, 128), f32),
            dma((3,)), pltpu.SemaphoreType.REGULAR,
            dma(()), dma(()), dma(()), dma((8,)), dma(()), dma(()),
            dma((4,)), dma((4,)),
        ],
        compiler_params=pltpu.CompilerParams(
            collective_id=0, has_side_effects=True, vmem_limit_bytes=32 * 2**20
        ),
        cost_estimate=pl.CostEstimate(flops=10**9, bytes_accessed=2**20, transcendentals=0),
    )(design_panel, sign_bits.reshape(1, 4096), sample_rows.reshape(1, 512))


def solution(mesh):
    return jax.shard_map(
        shards,
        mesh=mesh,
        in_specs=(P("cols", "rows"), P("rows"), P()),
        out_specs=P("cols", "rows"),
        check_vma=False,
    )
```

```python
import functools
import math

import jax
import jax.numpy as jnp
from jax import lax
from jax.experimental import pallas as pl
from jax.experimental.pallas import tpu as pltpu
from jax.sharding import PartitionSpec as P

MESH = pl.DeviceIdType.MESH
f32, bf16, i32 = jnp.float32, jnp.bfloat16, jnp.int32
HIGH = lax.Precision.HIGHEST
N_X, N_Z = 4, 16
PLANE = 8
HALVES = 2
PARTS = tuple(slice(8 // HALVES * n, 8 // HALVES * (n + 1)) for n in range(HALVES))
FAR = (6, 5, 7, 2, 4, 1, 3, 0)
NEAR = (0, 1, 3)


def parity(value, bits):
    shift = bits // 2
    while shift:
        value = value ^ (value >> shift)
        shift //= 2
    return value & 1


def sylvester(n):
    rows = lax.broadcasted_iota(i32, (n, n), 0)
    cols = lax.broadcasted_iota(i32, (n, n), 1)
    return (1 - 2 * parity(rows & cols, 8)).astype(f32).astype(bf16)


def parts(value):
    high = value.astype(bf16)
    rest = value - high.astype(f32)
    middle = rest.astype(bf16)
    low = (rest - middle.astype(f32)).astype(bf16)
    return high, middle, low


def exact_dot(value, table):
    high, middle, low = parts(value)
    dot = functools.partial(jnp.dot, preferred_element_type=f32)
    return dot(low, table) + dot(middle, table) + dot(high, table)


def butterflies(tiles):
    n, rows, _ = tiles.shape
    half = 1
    while half < n:
        pairs = tiles.reshape(n // (2 * half), 2, half, rows, 128)
        a, b = pairs[:, 0], pairs[:, 1]
        tiles = jnp.stack([a + b, a - b], axis=1).reshape(n, rows, 128)
        half *= 2
    return tiles


def wait_bytes(ref, sem):
    pltpu.make_async_copy(ref, ref, sem).wait()


def kernel(
    x_hbm, sign_hbm, sample_hbm, out_ref,
    x_ref, sign_ref, sample_ref,
    local, first, mixed, second, result,
    pick, pick_in, zsum, zsum_in, zrow, zall, picked, picked_all, factor,
    load_sem, go_sem,
    send_first, recv_first, send_second, recv_second, send_out, recv_out,
    chain_send, chain_recv,
):
    loads = [
        pltpu.make_async_copy(source, target, load_sem.at[n])
        for n, (source, target) in enumerate(
            ((x_hbm, x_ref), (sign_hbm, sign_ref), (sample_hbm, sample_ref))
        )
    ]
    for load in loads:
        load.start()

    p = lax.axis_index("rows")
    a = lax.axis_index("cols")
    z = lax.rem(p, N_Z)
    x = lax.rem(lax.div(p, N_Z), N_X)
    y = lax.div(p, N_Z * N_X)
    e = y * N_X + x
    quarter = lax.rem(x, 2) * 2 + lax.div(z, 8)
    slot = lax.rem(z, 8)
    block = y * 2 + lax.div(x, 2)
    plane = []
    for de in range(PLANE):
        plane.append(lax.rem(y + de // N_X, 2) * N_X + lax.rem(x + de % N_X, N_X))
    base = [at * N_Z for at in plane]
    col = [a] + [lax.rem(a + k, 4) for k in range(1, 4)]

    def along(dz):
        return lax.rem(z + dz, N_Z)

    def far_first(i):
        return 8 + lax.div(i + 1, 2) * (1 - 2 * lax.rem(i, 2))

    def even(i):
        middle = lax.div(i + 1, 2)
        return lax.rem(8 + middle * (2 * lax.rem(i, 2) - 1), 8)

    def remote(source, target, send, recv, row, column):
        pltpu.make_async_remote_copy(
            src_ref=source, dst_ref=target, send_sem=send, recv_sem=recv,
            device_id=(row, column), device_id_type=MESH,
        ).start()

    def signal(sem, row, column):
        pl.semaphore_signal(sem, inc=1, device_id=(row, column), device_id_type=MESH)

    barrier = pltpu.get_barrier_semaphore()

    def greet(i, carry):
        zz = along(far_first(i))
        for de in NEAR:
            signal(barrier, base[de] + zz, a)
        return carry

    lax.fori_loop(0, N_Z - 1, greet, 0, unroll=True)
    for de in range(1, PLANE):
        signal(barrier, base[de] + z, a)
    for k in range(1, 4):
        signal(barrier, p, col[k])

    for load in loads:
        load.wait()
    scale = f32(1.0 / math.sqrt(524288.0))
    signs = (2 * sign_ref[...] - 1).astype(f32) * scale
    table = sylvester(128)
    for cb in range(4):
        flipped = x_ref[cb * 8 : cb * 8 + 8, :] * signs
        tiles = jnp.concatenate([flipped[:, j * 128 : j * 128 + 128] for j in range(32)], axis=0)
        tiles = exact_dot(tiles, table).reshape(32, 8, 128)
        local[cb * 32 : cb * 32 + 32] = butterflies(tiles)

    samples = sample_ref[...]
    hot = (lax.broadcasted_iota(i32, (128, 512), 0) == lax.rem(samples, 128)).astype(f32).astype(bf16)
    want = jnp.broadcast_to(lax.rem(lax.div(samples, 128), 32), (8, 512))
    flip = (1 - 2 * parity(lax.div(samples, 4096) & p, 8)).astype(f32)
    for cb in range(4):
        chosen = exact_dot(local[cb * 32 : cb * 32 + 32].reshape(256, 128), hot)
        total = jnp.zeros((8, 512), f32)
        for j in range(32):
            total = jnp.where(want == j, chosen[j * 8 : j * 8 + 8], total)
        total = total * flip
        for hf in range(2):
            for h in range(2):
                at = (hf * 2 + h) * 128
                pick[cb * 2 + hf, h] = total[:, at : at + 128]

    pl.semaphore_wait(barrier, (N_Z - 1) * len(NEAR) + PLANE - 1 + 3)

    def greet_again(i, carry):
        signal(go_sem, base[0] + along(far_first(i)), a)
        return carry

    lax.fori_loop(0, N_Z - 1, greet_again, 0, unroll=True)

    for de in range(1, PLANE):
        remote(pick.at[plane[de]], pick_in.at[e], chain_send.at[0], chain_recv.at[0], base[de] + z, a)

    def send_tile(row, n):
        remote(local.at[row, PARTS[n]], first.at[p, PARTS[n]], send_first, recv_first.at[n], row, a)

    def send_tiles(n, some):
        def send_plane(i, carry):
            zz = along(far_first(i))
            for de in some:
                send_tile(base[de] + zz, n)
            return carry

        return send_plane

    others = tuple(de for de in FAR if de not in NEAR)
    lax.fori_loop(0, N_Z - 1, send_tiles(0, NEAR), 0, unroll=3)
    for de in FAR[:-1]:
        send_tile(base[de] + z, 0)
    pl.semaphore_wait(go_sem, N_Z - 1)
    first[p] = local[p]
    pick_in[e] = pick[e]

    lax.fori_loop(0, N_Z - 1, send_tiles(0, others), 0)

    wait_bytes(pick_in.at[pl.ds(0, PLANE - 1)], chain_recv.at[0])
    share = jnp.sum(pick_in[...], axis=0)
    for r in range(16):
        zsum[r] = share[r // 8, r % 8 : r % 8 + 1, :]

    def send_zsum(i, carry):
        zz = along(far_first(i))
        remote(zsum.at[zz], zsum_in.at[z], chain_send.at[1], chain_recv.at[1], base[0] + zz, a)
        return carry

    lax.fori_loop(0, N_Z - 1, send_zsum, 0, unroll=True)
    zsum_in[z] = zsum[z]
    lax.fori_loop(0, 8, send_tiles(1, FAR), 0)
    wait_bytes(zsum_in.at[pl.ds(0, N_Z - 1)], chain_recv.at[1])
    row_sum = jnp.sum(zsum_in[...], axis=0)
    zrow[0] = row_sum
    zall[z] = row_sum

    def send_zrow(i, carry):
        remote(zrow.at[0], zall.at[z], chain_send.at[2], chain_recv.at[2], base[0] + along(far_first(i)), a)
        return carry

    lax.fori_loop(0, N_Z - 1, send_zrow, 0, unroll=True)
    lax.fori_loop(8, N_Z - 1, send_tiles(1, FAR), 0)
    for de in FAR[:-1]:
        send_tile(base[de] + z, 1)

    mine = lax.rem(e, 2) * 16 + a * 4 + lax.div(e, 2)

    def share_picked():
        wait_bytes(zall.at[pl.ds(0, N_Z - 1)], chain_recv.at[2])
        for h in range(2):
            picked[h] = jnp.concatenate([zall[h * 8 + r] for r in range(8)], axis=0)
        for de in range(PLANE):
            for k in range(4):
                if de or k:
                    remote(
                        picked, picked_all.at[mine], chain_send.at[3], chain_recv.at[3],
                        base[de] + z, col[k],
                    )
        picked_all[mine] = picked[...]

    landed = recv_second.at[slot]
    away = quarter != a

    def mix_and_send(n, zz, own):
        part = PARTS[n]
        target = second.at[slot, a * 4 + block, part]
        tiles = butterflies(jnp.stack([first[hi * 16 + zz, part] for hi in range(PLANE)], axis=0))
        for hi in range(PLANE):
            mixed[hi * 16 + zz, part] = tiles[hi]
        for de in FAR[: PLANE - own]:
            remote(mixed.at[base[de] + zz, part], target, send_second, landed, base[de] + zz, quarter)
        if own:

            @pl.when(away)
            def _():
                remote(mixed.at[p, part], target, send_second, landed, p, quarter)

            @pl.when(jnp.logical_not(away))
            def _():
                pltpu.make_async_copy(mixed.at[p, part], target, landed).start()

    for n in range(HALVES):
        part = PARTS[n]
        wait_bytes(first.at[pl.ds(0, 127), part], recv_first.at[n])
        for hi in range(PLANE):
            first[hi * 16 : hi * 16 + 16, part] = butterflies(first[hi * 16 : hi * 16 + 16, part])

        def send_mixed(i, carry):
            mix_and_send(n, along(even(i)), False)
            mix_and_send(n, along(even(i) + 8), False)
            return carry

        mix_and_send(n, along(8), False)
        mix_and_send(n, z, True)
        lax.fori_loop(1, 8, send_mixed, 0)
        if n == 0:
            share_picked()

    wait_bytes(picked_all.at[pl.ds(0, 31)], chain_recv.at[3])
    gram = jnp.zeros((128, 128), f32)
    for hf in range(2):
        for h in range(2):
            part = picked_all[hf * 16 : hf * 16 + 16, h].reshape(128, 128)
            gram = gram + lax.dot_general(
                part, part, (((1,), (1,)), ((), ())), precision=HIGH, preferred_element_type=f32
            )
    gram = gram * f32(1.0 / 512.0)
    rows = lax.broadcasted_iota(i32, (128, 128), 0)
    cols = lax.broadcasted_iota(i32, (128, 128), 1)
    eye = (rows == cols).astype(f32)
    rest = jnp.concatenate([gram, eye], axis=1)
    for b in range(16):
        place = lax.broadcasted_iota(i32, (128 - 8 * b, 1), 0)
        for r in range(8):
            k = b * 8 + r
            pivot_row = rest[r : r + 1, :]
            pivot_row = pivot_row * (1.0 / pivot_row[:, k : k + 1])
            below = jnp.where(place > r, rest[:, k : k + 1], 0.0)
            rest = rest - below * pivot_row
        done = rest[:8]
        pivots = jnp.sum(jnp.where(eye[b * 8 : b * 8 + 8] > 0, done[:, :128], 0.0), axis=1, keepdims=True)
        factor[b * 8 : b * 8 + 8] = done[:, 128:] * lax.rsqrt(pivots)
        rest = rest[8:]

    inverse = factor[...]

    def finish(step, carry):
        at = lax.rem(z + 8 - even(step), 8)
        wait_bytes(second.at[at], recv_second.at[at])
        value = jnp.dot(
            inverse, second[at].reshape(128, 128), precision=HIGH, preferred_element_type=f32
        )
        result[at] = value.reshape(4, 32, 128)
        start = pl.multiple_of((a * 8 + at) * 128, 128)
        there = out_ref.at[:, pl.ds(start, 128)]
        for k in range(1, 4):
            remote(result.at[at, col[k]], there, send_out, recv_out, p, col[k])
        pltpu.make_async_copy(result.at[at, a], there, recv_out).start()
        return carry

    lax.fori_loop(0, 8, finish, 0)

    wait_bytes(out_ref, recv_out)
    wait_bytes(local.at[pl.ds(0, 127)], send_first)
    wait_bytes(mixed.at[pl.ds(0, 127)], send_second)

    @pl.when(away)
    def _():
        wait_bytes(mixed.at[0], send_second)

    wait_bytes(result.at[pl.ds(0, 6)], send_out)
    wait_bytes(pick.at[pl.ds(0, PLANE - 1)], chain_send.at[0])
    wait_bytes(zsum.at[pl.ds(0, N_Z - 1)], chain_send.at[1])
    wait_bytes(zall.at[pl.ds(0, N_Z - 1)], chain_send.at[2])
    wait_bytes(picked_all.at[pl.ds(0, 31)], chain_send.at[3])


def shards(design_panel, sign_bits, sample_rows):
    anywhere = pl.BlockSpec(memory_space=pl.ANY)
    tiles = pltpu.VMEM((128, 8, 128), f32)
    dma = pltpu.SemaphoreType.DMA
    return pl.pallas_call(
        kernel,
        out_shape=jax.ShapeDtypeStruct((32, 4096), f32),
        in_specs=[anywhere] * 3,
        out_specs=anywhere,
        scratch_shapes=[
            pltpu.VMEM((32, 4096), f32),
            pltpu.VMEM((1, 4096), i32),
            pltpu.VMEM((1, 512), i32),
            tiles, tiles, tiles,
            pltpu.VMEM((8, 16, 8, 128), f32),
            pltpu.VMEM((8, 4, 32, 128), f32),
            pltpu.VMEM((8, 2, 8, 128), f32),
            pltpu.VMEM((8, 2, 8, 128), f32),
            pltpu.VMEM((16, 1, 128), f32),
            pltpu.VMEM((16, 1, 128), f32),
            pltpu.VMEM((1, 1, 128), f32),
            pltpu.VMEM((16, 1, 128), f32),
            pltpu.VMEM((2, 8, 128), f32),
            pltpu.VMEM((32, 2, 8, 128), f32),
            pltpu.VMEM((128, 128), f32),
            dma((3,)), pltpu.SemaphoreType.REGULAR,
            dma(()), dma((HALVES,)), dma(()), dma((8,)), dma(()), dma(()),
            dma((4,)), dma((4,)),
        ],
        compiler_params=pltpu.CompilerParams(
            collective_id=0, has_side_effects=True, vmem_limit_bytes=32 * 2**20
        ),
        cost_estimate=pl.CostEstimate(flops=10**9, bytes_accessed=2**20, transcendentals=0),
    )(design_panel, sign_bits.reshape(1, 4096), sample_rows.reshape(1, 512))


def solution(mesh):
    return jax.shard_map(
        shards,
        mesh=mesh,
        in_specs=(P("cols", "rows"), P("rows"), P()),
        out_specs=P("cols", "rows"),
        check_vma=False,
    )
```

```python
import functools
import math

import jax
import jax.numpy as jnp
from jax import lax
from jax.experimental import pallas as pl
from jax.experimental.pallas import tpu as pltpu
from jax.sharding import PartitionSpec as P

MESH = pl.DeviceIdType.MESH
f32, bf16, i32 = jnp.float32, jnp.bfloat16, jnp.int32
HIGH = lax.Precision.HIGHEST
N_X, N_Z = 4, 16
PLANE = 8
HALVES = 2
PARTS = tuple(slice(8 // HALVES * n, 8 // HALVES * (n + 1)) for n in range(HALVES))
FAR = (6, 5, 7, 2, 4, 1, 3, 0)
NEAR = (0, 1, 3)
CLOSE = (4, 12, 3, 13, 2, 14, 1, 15)
DISTANT = (8, 7, 9, 6, 10, 5, 11)


def parity(value, bits):
    shift = bits // 2
    while shift:
        value = value ^ (value >> shift)
        shift //= 2
    return value & 1


def sylvester(n):
    rows = lax.broadcasted_iota(i32, (n, n), 0)
    cols = lax.broadcasted_iota(i32, (n, n), 1)
    return (1 - 2 * parity(rows & cols, 8)).astype(f32).astype(bf16)


def parts(value):
    high = value.astype(bf16)
    rest = value - high.astype(f32)
    middle = rest.astype(bf16)
    low = (rest - middle.astype(f32)).astype(bf16)
    return high, middle, low


def exact_dot(value, table):
    high, middle, low = parts(value)
    dot = functools.partial(jnp.dot, preferred_element_type=f32)
    return dot(low, table) + dot(middle, table) + dot(high, table)


def butterflies(tiles):
    n, rows, _ = tiles.shape
    half = 1
    while half < n:
        pairs = tiles.reshape(n // (2 * half), 2, half, rows, 128)
        a, b = pairs[:, 0], pairs[:, 1]
        tiles = jnp.stack([a + b, a - b], axis=1).reshape(n, rows, 128)
        half *= 2
    return tiles


def wait_bytes(ref, sem):
    pltpu.make_async_copy(ref, ref, sem).wait()


def kernel(
    x_hbm, sign_hbm, sample_hbm, out_ref,
    x_ref, sign_ref, sample_ref,
    local, first, mixed, second, result,
    pick, pick_in, zsum, zsum_in, zrow, zall, picked, picked_all, factor,
    load_sem, go_sem,
    send_first, recv_first, send_second, recv_second, send_out, recv_out,
    chain_send, chain_recv,
):
    loads = [
        pltpu.make_async_copy(source, target, load_sem.at[n])
        for n, (source, target) in enumerate(
            ((x_hbm, x_ref), (sign_hbm, sign_ref), (sample_hbm, sample_ref))
        )
    ]
    for load in loads:
        load.start()

    p = lax.axis_index("rows")
    a = lax.axis_index("cols")
    z = lax.rem(p, N_Z)
    x = lax.rem(lax.div(p, N_Z), N_X)
    y = lax.div(p, N_Z * N_X)
    e = y * N_X + x
    quarter = lax.rem(x, 2) * 2 + lax.div(z, 8)
    slot = lax.rem(z, 8)
    block = y * 2 + lax.div(x, 2)
    plane = []
    for de in range(PLANE):
        plane.append(lax.rem(y + de // N_X, 2) * N_X + lax.rem(x + de % N_X, N_X))
    base = [at * N_Z for at in plane]
    col = [a] + [lax.rem(a + k, 4) for k in range(1, 4)]

    def along(dz):
        return lax.rem(z + dz, N_Z)

    def far_first(i):
        return 8 + lax.div(i + 1, 2) * (1 - 2 * lax.rem(i, 2))

    def even(i):
        middle = lax.div(i + 1, 2)
        return lax.rem(8 + middle * (2 * lax.rem(i, 2) - 1), 8)

    def remote(source, target, send, recv, row, column):
        pltpu.make_async_remote_copy(
            src_ref=source, dst_ref=target, send_sem=send, recv_sem=recv,
            device_id=(row, column), device_id_type=MESH,
        ).start()

    def signal(sem, row, column):
        pl.semaphore_signal(sem, inc=1, device_id=(row, column), device_id_type=MESH)

    barrier = pltpu.get_barrier_semaphore()

    for dz in CLOSE:
        for de in NEAR:
            signal(barrier, base[de] + along(dz), a)
    for de in range(1, PLANE):
        signal(barrier, base[de] + z, a)
    for k in range(1, 4):
        signal(barrier, p, col[k])

    for load in loads:
        load.wait()
    scale = f32(1.0 / math.sqrt(524288.0))
    signs = (2 * sign_ref[...] - 1).astype(f32) * scale
    table = sylvester(128)
    for cb in range(4):
        flipped = x_ref[cb * 8 : cb * 8 + 8, :] * signs
        tiles = jnp.concatenate([flipped[:, j * 128 : j * 128 + 128] for j in range(32)], axis=0)
        tiles = exact_dot(tiles, table).reshape(32, 8, 128)
        local[cb * 32 : cb * 32 + 32] = butterflies(tiles)

    samples = sample_ref[...]
    hot = (lax.broadcasted_iota(i32, (128, 512), 0) == lax.rem(samples, 128)).astype(f32).astype(bf16)
    want = jnp.broadcast_to(lax.rem(lax.div(samples, 128), 32), (8, 512))
    flip = (1 - 2 * parity(lax.div(samples, 4096) & p, 8)).astype(f32)
    for cb in range(4):
        chosen = exact_dot(local[cb * 32 : cb * 32 + 32].reshape(256, 128), hot)
        total = jnp.zeros((8, 512), f32)
        for j in range(32):
            total = jnp.where(want == j, chosen[j * 8 : j * 8 + 8], total)
        total = total * flip
        for hf in range(2):
            for h in range(2):
                at = (hf * 2 + h) * 128
                pick[cb * 2 + hf, h] = total[:, at : at + 128]

    pl.semaphore_wait(barrier, len(CLOSE) * len(NEAR) + PLANE - 1 + 3)

    def tell(sem):
        for dz in CLOSE:
            signal(sem, base[0] + along(dz), a)

    tell(go_sem.at[0])

    for de in range(1, PLANE):
        remote(pick.at[plane[de]], pick_in.at[e], chain_send.at[0], chain_recv.at[0], base[de] + z, a)

    def send_tile(row, n):
        remote(local.at[row, PARTS[n]], first.at[p, PARTS[n]], send_first, recv_first.at[n], row, a)

    def send_tiles(n, steps, some):
        for dz in steps:
            zz = along(dz)
            for de in some:
                send_tile(base[de] + zz, n)

    others = tuple(de for de in FAR if de not in NEAR)
    send_tiles(0, CLOSE, NEAR)
    for de in FAR[:-1]:
        send_tile(base[de] + z, 0)
    send_tiles(1, CLOSE, NEAR)
    pl.semaphore_wait(go_sem.at[0], len(CLOSE))
    tell(go_sem.at[1])
    send_tiles(0, CLOSE, others)
    send_tiles(0, DISTANT, NEAR)
    pl.semaphore_wait(go_sem.at[1], len(CLOSE))
    send_tiles(0, DISTANT, others)
    first[p] = local[p]
    pick_in[e] = pick[e]


    wait_bytes(pick_in.at[pl.ds(0, PLANE - 1)], chain_recv.at[0])
    share = jnp.sum(pick_in[...], axis=0)
    for r in range(16):
        zsum[r] = share[r // 8, r % 8 : r % 8 + 1, :]

    def send_zsum(i, carry):
        zz = along(far_first(i))
        remote(zsum.at[zz], zsum_in.at[z], chain_send.at[1], chain_recv.at[1], base[0] + zz, a)
        return carry

    lax.fori_loop(0, N_Z - 1, send_zsum, 0, unroll=True)
    zsum_in[z] = zsum[z]
    send_tiles(1, DISTANT, FAR)
    wait_bytes(zsum_in.at[pl.ds(0, N_Z - 1)], chain_recv.at[1])
    row_sum = jnp.sum(zsum_in[...], axis=0)
    zrow[0] = row_sum
    zall[z] = row_sum

    def send_zrow(i, carry):
        remote(zrow.at[0], zall.at[z], chain_send.at[2], chain_recv.at[2], base[0] + along(far_first(i)), a)
        return carry

    lax.fori_loop(0, N_Z - 1, send_zrow, 0, unroll=True)
    send_tiles(1, CLOSE, others)
    for de in FAR[:-1]:
        send_tile(base[de] + z, 1)

    mine = lax.rem(e, 2) * 16 + a * 4 + lax.div(e, 2)

    def share_picked():
        wait_bytes(zall.at[pl.ds(0, N_Z - 1)], chain_recv.at[2])
        for h in range(2):
            picked[h] = jnp.concatenate([zall[h * 8 + r] for r in range(8)], axis=0)
        for de in range(PLANE):
            for k in range(4):
                if de or k:
                    remote(
                        picked, picked_all.at[mine], chain_send.at[3], chain_recv.at[3],
                        base[de] + z, col[k],
                    )
        picked_all[mine] = picked[...]

    landed = recv_second.at[slot]
    away = quarter != a

    def mix_and_send(n, zz, own):
        part = PARTS[n]
        target = second.at[slot, a * 4 + block, part]
        tiles = butterflies(jnp.stack([first[hi * 16 + zz, part] for hi in range(PLANE)], axis=0))
        for hi in range(PLANE):
            mixed[hi * 16 + zz, part] = tiles[hi]
        for de in FAR[: PLANE - own]:
            remote(mixed.at[base[de] + zz, part], target, send_second, landed, base[de] + zz, quarter)
        if own:

            @pl.when(away)
            def _():
                remote(mixed.at[p, part], target, send_second, landed, p, quarter)

            @pl.when(jnp.logical_not(away))
            def _():
                pltpu.make_async_copy(mixed.at[p, part], target, landed).start()

    for n in range(HALVES):
        part = PARTS[n]
        wait_bytes(first.at[pl.ds(0, 127), part], recv_first.at[n])
        for hi in range(PLANE):
            first[hi * 16 : hi * 16 + 16, part] = butterflies(first[hi * 16 : hi * 16 + 16, part])

        def send_mixed(i, carry):
            mix_and_send(n, along(even(i)), False)
            mix_and_send(n, along(even(i) + 8), False)
            return carry

        mix_and_send(n, along(8), False)
        mix_and_send(n, z, True)
        lax.fori_loop(1, 8, send_mixed, 0)
        if n == 0:
            share_picked()

    wait_bytes(picked_all.at[pl.ds(0, 31)], chain_recv.at[3])
    gram = jnp.zeros((128, 128), f32)
    for hf in range(2):
        for h in range(2):
            part = picked_all[hf * 16 : hf * 16 + 16, h].reshape(128, 128)
            gram = gram + lax.dot_general(
                part, part, (((1,), (1,)), ((), ())), precision=HIGH, preferred_element_type=f32
            )
    gram = gram * f32(1.0 / 512.0)
    rows = lax.broadcasted_iota(i32, (128, 128), 0)
    cols = lax.broadcasted_iota(i32, (128, 128), 1)
    eye = (rows == cols).astype(f32)
    rest = jnp.concatenate([gram, eye], axis=1)
    for b in range(16):
        place = lax.broadcasted_iota(i32, (128 - 8 * b, 1), 0)
        for r in range(8):
            k = b * 8 + r
            pivot_row = rest[r : r + 1, :]
            pivot_row = pivot_row * (1.0 / pivot_row[:, k : k + 1])
            below = jnp.where(place > r, rest[:, k : k + 1], 0.0)
            rest = rest - below * pivot_row
        done = rest[:8]
        pivots = jnp.sum(jnp.where(eye[b * 8 : b * 8 + 8] > 0, done[:, :128], 0.0), axis=1, keepdims=True)
        factor[b * 8 : b * 8 + 8] = done[:, 128:] * lax.rsqrt(pivots)
        rest = rest[8:]

    inverse = factor[...]

    def finish(step, carry):
        at = lax.rem(z + 8 - even(step), 8)
        wait_bytes(second.at[at], recv_second.at[at])
        value = jnp.dot(
            inverse, second[at].reshape(128, 128), precision=HIGH, preferred_element_type=f32
        )
        result[at] = value.reshape(4, 32, 128)
        start = pl.multiple_of((a * 8 + at) * 128, 128)
        there = out_ref.at[:, pl.ds(start, 128)]
        for k in range(1, 4):
            remote(result.at[at, col[k]], there, send_out, recv_out, p, col[k])
        pltpu.make_async_copy(result.at[at, a], there, recv_out).start()
        return carry

    lax.fori_loop(0, 8, finish, 0)

    wait_bytes(out_ref, recv_out)
    wait_bytes(local.at[pl.ds(0, 127)], send_first)
    wait_bytes(mixed.at[pl.ds(0, 127)], send_second)

    @pl.when(away)
    def _():
        wait_bytes(mixed.at[0], send_second)

    wait_bytes(result.at[pl.ds(0, 6)], send_out)
    wait_bytes(pick.at[pl.ds(0, PLANE - 1)], chain_send.at[0])
    wait_bytes(zsum.at[pl.ds(0, N_Z - 1)], chain_send.at[1])
    wait_bytes(zall.at[pl.ds(0, N_Z - 1)], chain_send.at[2])
    wait_bytes(picked_all.at[pl.ds(0, 31)], chain_send.at[3])


def shards(design_panel, sign_bits, sample_rows):
    anywhere = pl.BlockSpec(memory_space=pl.ANY)
    tiles = pltpu.VMEM((128, 8, 128), f32)
    dma = pltpu.SemaphoreType.DMA
    return pl.pallas_call(
        kernel,
        out_shape=jax.ShapeDtypeStruct((32, 4096), f32),
        in_specs=[anywhere] * 3,
        out_specs=anywhere,
        scratch_shapes=[
            pltpu.VMEM((32, 4096), f32),
            pltpu.VMEM((1, 4096), i32),
            pltpu.VMEM((1, 512), i32),
            tiles, tiles, tiles,
            pltpu.VMEM((8, 16, 8, 128), f32),
            pltpu.VMEM((8, 4, 32, 128), f32),
            pltpu.VMEM((8, 2, 8, 128), f32),
            pltpu.VMEM((8, 2, 8, 128), f32),
            pltpu.VMEM((16, 1, 128), f32),
            pltpu.VMEM((16, 1, 128), f32),
            pltpu.VMEM((1, 1, 128), f32),
            pltpu.VMEM((16, 1, 128), f32),
            pltpu.VMEM((2, 8, 128), f32),
            pltpu.VMEM((32, 2, 8, 128), f32),
            pltpu.VMEM((128, 128), f32),
            dma((3,)), pltpu.SemaphoreType.REGULAR((2,)),
            dma(()), dma((HALVES,)), dma(()), dma((8,)), dma(()), dma(()),
            dma((4,)), dma((4,)),
        ],
        compiler_params=pltpu.CompilerParams(
            collective_id=0, has_side_effects=True, vmem_limit_bytes=32 * 2**20
        ),
        cost_estimate=pl.CostEstimate(flops=10**9, bytes_accessed=2**20, transcendentals=0),
    )(design_panel, sign_bits.reshape(1, 4096), sample_rows.reshape(1, 512))


def solution(mesh):
    return jax.shard_map(
        shards,
        mesh=mesh,
        in_specs=(P("cols", "rows"), P("rows"), P()),
        out_specs=P("cols", "rows"),
        check_vma=False,
    )
```

```python
import functools
import math

import jax
import jax.numpy as jnp
from jax import lax
from jax.experimental import pallas as pl
from jax.experimental.pallas import tpu as pltpu
from jax.sharding import PartitionSpec as P

MESH = pl.DeviceIdType.MESH
f32, bf16, i32 = jnp.float32, jnp.bfloat16, jnp.int32
HIGH = lax.Precision.HIGHEST
N_X, N_Z = 4, 16
PLANE = 8
HALVES = 2
PARTS = tuple(slice(8 // HALVES * n, 8 // HALVES * (n + 1)) for n in range(HALVES))
FAR = (6, 5, 7, 2, 4, 1, 3, 0)
NEAR = (0, 1, 3)
CLOSE = (4, 12, 3, 13, 2, 14, 1, 15)
DISTANT = (8, 7, 9, 6, 10, 5, 11)


def parity(value, bits):
    shift = bits // 2
    while shift:
        value = value ^ (value >> shift)
        shift //= 2
    return value & 1


def sylvester(n):
    rows = lax.broadcasted_iota(i32, (n, n), 0)
    cols = lax.broadcasted_iota(i32, (n, n), 1)
    return (1 - 2 * parity(rows & cols, 8)).astype(f32).astype(bf16)


def parts(value):
    high = value.astype(bf16)
    rest = value - high.astype(f32)
    middle = rest.astype(bf16)
    low = (rest - middle.astype(f32)).astype(bf16)
    return high, middle, low


def exact_dot(value, table):
    high, middle, low = parts(value)
    dot = functools.partial(jnp.dot, preferred_element_type=f32)
    return dot(low, table) + dot(middle, table) + dot(high, table)


def butterflies(tiles):
    n, rows, _ = tiles.shape
    half = 1
    while half < n:
        pairs = tiles.reshape(n // (2 * half), 2, half, rows, 128)
        a, b = pairs[:, 0], pairs[:, 1]
        tiles = jnp.stack([a + b, a - b], axis=1).reshape(n, rows, 128)
        half *= 2
    return tiles


def wait_bytes(ref, sem):
    pltpu.make_async_copy(ref, ref, sem).wait()


def kernel(
    x_hbm, sign_hbm, sample_hbm, out_ref,
    x_ref, sign_ref, sample_ref,
    local, first, mixed, second, result,
    pick, pick_in, zsum, zsum_in, zrow, zall, picked, picked_all, factor,
    load_sem, go_sem,
    send_first, recv_first, send_second, recv_second, send_out, recv_out,
    chain_send, chain_recv,
):
    loads = [
        pltpu.make_async_copy(source, target, load_sem.at[n])
        for n, (source, target) in enumerate(
            ((x_hbm, x_ref), (sign_hbm, sign_ref), (sample_hbm, sample_ref))
        )
    ]
    p = lax.axis_index("rows")
    a = lax.axis_index("cols")
    z = lax.rem(p, N_Z)
    x = lax.rem(lax.div(p, N_Z), N_X)
    y = lax.div(p, N_Z * N_X)
    e = y * N_X + x
    quarter = lax.rem(x, 2) * 2 + lax.div(z, 8)
    slot = lax.rem(z, 8)
    block = y * 2 + lax.div(x, 2)
    plane = []
    for de in range(PLANE):
        plane.append(lax.rem(y + de // N_X, 2) * N_X + lax.rem(x + de % N_X, N_X))
    base = [at * N_Z for at in plane]
    col = [a] + [lax.rem(a + k, 4) for k in range(1, 4)]

    def along(dz):
        return lax.rem(z + dz, N_Z)

    def far_first(i):
        return 8 + lax.div(i + 1, 2) * (1 - 2 * lax.rem(i, 2))

    def even(i):
        middle = lax.div(i + 1, 2)
        return lax.rem(8 + middle * (2 * lax.rem(i, 2) - 1), 8)

    def remote(source, target, send, recv, row, column):
        pltpu.make_async_remote_copy(
            src_ref=source, dst_ref=target, send_sem=send, recv_sem=recv,
            device_id=(row, column), device_id_type=MESH,
        ).start()

    def signal(sem, row, column):
        pl.semaphore_signal(sem, inc=1, device_id=(row, column), device_id_type=MESH)

    barrier = pltpu.get_barrier_semaphore()

    for dz in CLOSE:
        for de in NEAR:
            signal(barrier, base[de] + along(dz), a)
    for de in range(1, PLANE):
        signal(barrier, base[de] + z, a)
    for k in range(1, 4):
        signal(barrier, p, col[k])

    for load in loads:
        load.start()
    for load in loads:
        load.wait()
    scale = f32(1.0 / math.sqrt(524288.0))
    signs = (2 * sign_ref[...] - 1).astype(f32) * scale
    table = sylvester(128)
    for cb in range(4):
        flipped = x_ref[cb * 8 : cb * 8 + 8, :] * signs
        tiles = jnp.concatenate([flipped[:, j * 128 : j * 128 + 128] for j in range(32)], axis=0)
        tiles = exact_dot(tiles, table).reshape(32, 8, 128)
        local[cb * 32 : cb * 32 + 32] = butterflies(tiles)

    samples = sample_ref[...]
    hot = (lax.broadcasted_iota(i32, (128, 512), 0) == lax.rem(samples, 128)).astype(f32).astype(bf16)
    want = jnp.broadcast_to(lax.rem(lax.div(samples, 128), 32), (8, 512))
    flip = (1 - 2 * parity(lax.div(samples, 4096) & p, 8)).astype(f32)
    for cb in range(4):
        chosen = exact_dot(local[cb * 32 : cb * 32 + 32].reshape(256, 128), hot)
        total = jnp.zeros((8, 512), f32)
        for j in range(32):
            total = jnp.where(want == j, chosen[j * 8 : j * 8 + 8], total)
        total = total * flip
        for hf in range(2):
            for h in range(2):
                at = (hf * 2 + h) * 128
                pick[cb * 2 + hf, h] = total[:, at : at + 128]

    pl.semaphore_wait(barrier, len(CLOSE) * len(NEAR) + PLANE - 1 + 3)

    def tell(sem):
        for dz in CLOSE:
            signal(sem, base[0] + along(dz), a)

    tell(go_sem.at[0])

    for de in range(1, PLANE):
        remote(pick.at[plane[de]], pick_in.at[e], chain_send.at[0], chain_recv.at[0], base[de] + z, a)

    def send_tile(row, n):
        remote(local.at[row, PARTS[n]], first.at[p, PARTS[n]], send_first, recv_first.at[n], row, a)

    def send_tiles(n, steps, some):
        for dz in steps:
            zz = along(dz)
            for de in some:
                send_tile(base[de] + zz, n)

    others = tuple(de for de in FAR if de not in NEAR)
    send_tiles(0, CLOSE, NEAR)
    for de in FAR[:-1]:
        send_tile(base[de] + z, 0)
    send_tiles(1, CLOSE, NEAR)
    pl.semaphore_wait(go_sem.at[0], len(CLOSE))
    tell(go_sem.at[1])
    send_tiles(0, CLOSE, others)
    send_tiles(0, DISTANT, NEAR)
    pl.semaphore_wait(go_sem.at[1], len(CLOSE))
    send_tiles(0, DISTANT, others)
    first[p] = local[p]
    pick_in[e] = pick[e]


    wait_bytes(pick_in.at[pl.ds(0, PLANE - 1)], chain_recv.at[0])
    share = jnp.sum(pick_in[...], axis=0)
    for r in range(16):
        zsum[r] = share[r // 8, r % 8 : r % 8 + 1, :]

    def send_zsum(i, carry):
        zz = along(far_first(i))
        remote(zsum.at[zz], zsum_in.at[z], chain_send.at[1], chain_recv.at[1], base[0] + zz, a)
        return carry

    lax.fori_loop(0, N_Z - 1, send_zsum, 0, unroll=True)
    zsum_in[z] = zsum[z]
    send_tiles(1, DISTANT, FAR)
    wait_bytes(zsum_in.at[pl.ds(0, N_Z - 1)], chain_recv.at[1])
    row_sum = jnp.sum(zsum_in[...], axis=0)
    zrow[0] = row_sum
    zall[z] = row_sum

    def send_zrow(i, carry):
        remote(zrow.at[0], zall.at[z], chain_send.at[2], chain_recv.at[2], base[0] + along(far_first(i)), a)
        return carry

    lax.fori_loop(0, N_Z - 1, send_zrow, 0, unroll=True)
    send_tiles(1, CLOSE, others)
    for de in FAR[:-1]:
        send_tile(base[de] + z, 1)

    mine = lax.rem(e, 2) * 16 + a * 4 + lax.div(e, 2)

    def share_picked():
        wait_bytes(zall.at[pl.ds(0, N_Z - 1)], chain_recv.at[2])
        for h in range(2):
            picked[h] = jnp.concatenate([zall[h * 8 + r] for r in range(8)], axis=0)
        for de in range(PLANE):
            for k in range(4):
                if de or k:
                    remote(
                        picked, picked_all.at[mine], chain_send.at[3], chain_recv.at[3],
                        base[de] + z, col[k],
                    )
        picked_all[mine] = picked[...]

    landed = recv_second.at[slot]
    away = quarter != a

    def mix_and_send(n, zz, own):
        part = PARTS[n]
        target = second.at[slot, a * 4 + block, part]
        tiles = butterflies(jnp.stack([first[hi * 16 + zz, part] for hi in range(PLANE)], axis=0))
        for hi in range(PLANE):
            mixed[hi * 16 + zz, part] = tiles[hi]
        for de in FAR[: PLANE - own]:
            remote(mixed.at[base[de] + zz, part], target, send_second, landed, base[de] + zz, quarter)
        if own:

            @pl.when(away)
            def _():
                remote(mixed.at[p, part], target, send_second, landed, p, quarter)

            @pl.when(jnp.logical_not(away))
            def _():
                pltpu.make_async_copy(mixed.at[p, part], target, landed).start()

    for n in range(HALVES):
        part = PARTS[n]
        wait_bytes(first.at[pl.ds(0, 127), part], recv_first.at[n])
        for hi in range(PLANE):
            first[hi * 16 : hi * 16 + 16, part] = butterflies(first[hi * 16 : hi * 16 + 16, part])

        def send_mixed(i, carry):
            mix_and_send(n, along(even(i)), False)
            mix_and_send(n, along(even(i) + 8), False)
            return carry

        mix_and_send(n, along(8), False)
        mix_and_send(n, z, True)
        lax.fori_loop(1, 8, send_mixed, 0)
        if n == 0:
            share_picked()

    wait_bytes(picked_all.at[pl.ds(0, 31)], chain_recv.at[3])
    gram = jnp.zeros((128, 128), f32)
    for hf in range(2):
        for h in range(2):
            part = picked_all[hf * 16 : hf * 16 + 16, h].reshape(128, 128)
            gram = gram + lax.dot_general(
                part, part, (((1,), (1,)), ((), ())), precision=HIGH, preferred_element_type=f32
            )
    gram = gram * f32(1.0 / 512.0)
    rows = lax.broadcasted_iota(i32, (128, 128), 0)
    cols = lax.broadcasted_iota(i32, (128, 128), 1)
    eye = (rows == cols).astype(f32)
    rest = jnp.concatenate([gram, eye], axis=1)
    for b in range(16):
        place = lax.broadcasted_iota(i32, (128 - 8 * b, 1), 0)
        for r in range(8):
            k = b * 8 + r
            pivot_row = rest[r : r + 1, :]
            pivot_row = pivot_row * (1.0 / pivot_row[:, k : k + 1])
            below = jnp.where(place > r, rest[:, k : k + 1], 0.0)
            rest = rest - below * pivot_row
        done = rest[:8]
        pivots = jnp.sum(jnp.where(eye[b * 8 : b * 8 + 8] > 0, done[:, :128], 0.0), axis=1, keepdims=True)
        factor[b * 8 : b * 8 + 8] = done[:, 128:] * lax.rsqrt(pivots)
        rest = rest[8:]

    inverse = factor[...]

    def finish(step, carry):
        at = lax.rem(z + 8 - even(step), 8)
        wait_bytes(second.at[at], recv_second.at[at])
        value = jnp.dot(
            inverse, second[at].reshape(128, 128), precision=HIGH, preferred_element_type=f32
        )
        result[at] = value.reshape(4, 32, 128)
        start = pl.multiple_of((a * 8 + at) * 128, 128)
        there = out_ref.at[:, pl.ds(start, 128)]
        for k in range(1, 4):
            remote(result.at[at, col[k]], there, send_out, recv_out, p, col[k])
        pltpu.make_async_copy(result.at[at, a], there, recv_out).start()
        return carry

    lax.fori_loop(0, 8, finish, 0)

    wait_bytes(out_ref, recv_out)
    wait_bytes(local.at[pl.ds(0, 127)], send_first)
    wait_bytes(mixed.at[pl.ds(0, 127)], send_second)

    @pl.when(away)
    def _():
        wait_bytes(mixed.at[0], send_second)

    wait_bytes(result.at[pl.ds(0, 6)], send_out)
    wait_bytes(pick.at[pl.ds(0, PLANE - 1)], chain_send.at[0])
    wait_bytes(zsum.at[pl.ds(0, N_Z - 1)], chain_send.at[1])
    wait_bytes(zall.at[pl.ds(0, N_Z - 1)], chain_send.at[2])
    wait_bytes(picked_all.at[pl.ds(0, 31)], chain_send.at[3])


def shards(design_panel, sign_bits, sample_rows):
    anywhere = pl.BlockSpec(memory_space=pl.ANY)
    tiles = pltpu.VMEM((128, 8, 128), f32)
    dma = pltpu.SemaphoreType.DMA
    return pl.pallas_call(
        kernel,
        out_shape=jax.ShapeDtypeStruct((32, 4096), f32),
        in_specs=[anywhere] * 3,
        out_specs=pl.BlockSpec(memory_space=pltpu.VMEM),
        scratch_shapes=[
            pltpu.VMEM((32, 4096), f32),
            pltpu.VMEM((1, 4096), i32),
            pltpu.VMEM((1, 512), i32),
            tiles, tiles, tiles,
            pltpu.VMEM((8, 16, 8, 128), f32),
            pltpu.VMEM((8, 4, 32, 128), f32),
            pltpu.VMEM((8, 2, 8, 128), f32),
            pltpu.VMEM((8, 2, 8, 128), f32),
            pltpu.VMEM((16, 1, 128), f32),
            pltpu.VMEM((16, 1, 128), f32),
            pltpu.VMEM((1, 1, 128), f32),
            pltpu.VMEM((16, 1, 128), f32),
            pltpu.VMEM((2, 8, 128), f32),
            pltpu.VMEM((32, 2, 8, 128), f32),
            pltpu.VMEM((128, 128), f32),
            dma((3,)), pltpu.SemaphoreType.REGULAR((2,)),
            dma(()), dma((HALVES,)), dma(()), dma((8,)), dma(()), dma(()),
            dma((4,)), dma((4,)),
        ],
        compiler_params=pltpu.CompilerParams(
            collective_id=0, has_side_effects=True, vmem_limit_bytes=32 * 2**20
        ),
        cost_estimate=pl.CostEstimate(flops=10**9, bytes_accessed=2**20, transcendentals=0),
    )(design_panel, sign_bits.reshape(1, 4096), sample_rows.reshape(1, 512))


def solution(mesh):
    return jax.shard_map(
        shards,
        mesh=mesh,
        in_specs=(P("cols", "rows"), P("rows"), P()),
        out_specs=P("cols", "rows"),
        check_vma=False,
    )
```
